32 devices in a mesh: row: 8 (over z, y), col: 4 (over x, core).
Axes of the slice: x: 2, y: 2, z: 4, core: 2. Of those that a mesh axis runs over, the one named last changes fastest.
Arguments:
- start_values: float32 [44, 4, 2, 256], P(None, 'col', None, 'row'), may hold values from -6 to 6
- cosine: float32 [256], P('row'), may hold values from -0.99 to 0.99
- arc_index: int32 [256], P('row'), may hold values from 0 to 7, never falling along the last dimension, each value on 1 to 128 neighbouring positions
- arc_weight: float32 [8], replicated, may hold values from 0.003 to 0.03
- observed: float32 [256], P('row'), may hold values from -12 to 12
- orientation_term: float32 [256, 44, 4, 128], P('row', None, 'col'), may hold values from -3 to 3
- step_gain: float32 [44, 4, 128], replicated, may hold values from 1.5 to 1.9
- step_damp: float32 [44, 4, 128], replicated, may hold values from 0.94 to 1
Outputs:
- normal_update: float32 [4, 1024, 44, 512], P(None, 'row', None, 'col')
- rhs_update: float32 [44, 4, 128], P(None, 'col')
The draws below stay inside these ranges and needn't reach their ends.
Inputs may be any that keep to these rules, and one draw needn't show every extreme that they name: `arc_index`: Non-decreasing along the observations; each arc names 1 to 128 consecutive observations.
All inputs are finite; a program needn't handle non-finite values.
Results may differ from the reference program's by a relative error of at most 0.000073.
Values sent between devices are 32-bit elements; how exact they have to be, the bound alone decides.
A program may use at most 128 MiB of HBM per device.

```python
import math
import jax
import jax.numpy as jnp
import numpy as np
from jax import lax

NB = 128
CT = 44
RT = 4
ARCS = 8
OBS = 256
SLAB = 4096
N_ROW = 8
N_COL = 4


def steps_of(rng, dims, pieces, least, largest):
    loudness = 1.0
    for axis_at, shards_of in pieces:
        steps = jax.random.uniform(jax.random.fold_in(jax.random.fold_in(rng, 6), axis_at), (shards_of,), jnp.float32, least / len(pieces), largest / len(pieces))
        loudness = loudness * jnp.repeat(jnp.exp(steps), dims[axis_at] // shards_of).reshape((-1,) + (1,) * (len(dims) - 1 - axis_at))
    return loudness


def length_profile(count, total, limit, slope):
    loads = [(1 << 20) // math.isqrt(standing ** slope) + 1 for standing in range(2, count + 1)]
    spare, counts = total - limit - (count - 1), [1] * (count - 1)
    while spare > 0:
        movable = [i for i in range(count - 1) if counts[i] < limit]
        pool, remaining = sum([loads[i] for i in movable]), spare
        for i in movable:
            more = min(limit - counts[i], max(1, remaining * loads[i] // pool), spare)
            counts[i] = counts[i] + more
            spare = spare - more
    return np.array([limit] + counts)


def ragged_sizes(rng, number_of, total, bound, skew):
    if number_of == 2:
        one = jax.random.randint(rng, (), max(1, total - bound), min(bound, total - 1) + 1)
        return jnp.stack([one, total - one])
    tallies = jnp.asarray(length_profile(number_of, total, bound, skew), jnp.int32)
    twos = (number_of - 1) // 2
    giver, sink = tallies[1:1 + 2 * twos:2], tallies[2:2 + 2 * twos:2]
    slack = jnp.minimum(giver - 1, bound - sink)
    shifted = jax.random.randint(jax.random.fold_in(rng, 1), (twos,), 0, 1 << 20) % (slack + 1)
    tallies = tallies.at[1:1 + 2 * twos:2].set(giver - shifted).at[2:2 + 2 * twos:2].set(sink + shifted)
    return tallies[jax.random.permutation(jax.random.fold_in(rng, 2), number_of)]


def scatter_about(key, dims, spread, reach, pieces=(), held_as=jnp.bfloat16):
    values = spread * jax.random.normal(key, dims, jnp.float32)
    if pieces:
        values = values * steps_of(key, dims, pieces, -0.22, 0.18)
    return jnp.clip(values, -reach, reach).astype(held_as)


def setup_inputs(seed: int = 0) -> dict:
    key_of = jax.random.split(jax.random.key(seed), 9)
    return {
        "start_values": scatter_about(key_of[0], (CT, N_COL, 2, OBS), 1.0, 6.0, ((1, 4), (3, 8)), jnp.float32),
        "cosine": jnp.clip(jax.random.uniform(key_of[1], (OBS,), jnp.float32, -0.99, 0.99) * steps_of(key_of[1], (OBS,), ((0, 8),), -0.4, 0.0), -0.99, 0.99),
        "arc_index": jnp.searchsorted(jnp.cumsum(ragged_sizes(key_of[2], ARCS, OBS, OBS // 2, 0)), jnp.arange(OBS), side="right").astype(jnp.int32),
        "arc_weight": jnp.clip(jnp.exp(jax.random.uniform(key_of[3], (ARCS,), jnp.float32, math.log(0.003), math.log(0.03))), 0.003, 0.03),
        "observed": scatter_about(key_of[4], (OBS,), 2.0, 12.0, ((0, 8),), jnp.float32),
        "orientation_term": scatter_about(key_of[5], (OBS, CT, N_COL, NB), 0.5, 3.0, ((0, 8), (2, 4)), jnp.float32),
        "step_gain": jnp.clip(jax.random.uniform(key_of[6], (CT, N_COL, NB), jnp.float32, 1.5, 1.9), 1.5, 1.9),
        "step_damp": jnp.clip(jax.random.uniform(key_of[7], (CT, N_COL, NB), jnp.float32, 0.94, 1.0), 0.94, 1.0),
    }


def legendre_tiles(start_values, cosine, forcing, step_gain, step_damp):
    def advance(state, factors):
        prev_two, prev_one = state
        gain_now, damp_now, force_now = factors
        current = (gain_now[:, None] * cosine[None, :]) * prev_one - damp_now[:, None] * prev_two + force_now
        return (prev_one, current), current

    initial = (start_values[:, 0, :], start_values[:, 1, :])
    force_steps = jnp.transpose(forcing, (2, 1, 0))
    final_state, columns = lax.scan(advance, initial, (step_gain.T, step_damp.T, force_steps), unroll=16)
    return jnp.transpose(columns, (2, 1, 0))


def reference(start_values, cosine, arc_index, arc_weight, observed, orientation_term, step_gain, step_damp):
    tile_total = CT * N_COL
    design = legendre_tiles(start_values.reshape(tile_total, 2, OBS), cosine,
                            orientation_term.reshape(OBS, tile_total, NB),
                            step_gain.reshape(tile_total, NB), step_damp.reshape(tile_total, NB))
    design = design.reshape(OBS, tile_total * NB)
    labels = jnp.arange(ARCS, dtype=jnp.int32)
    picked = (arc_index[:, None] == labels[None, :]).astype(jnp.float32)
    weight = jnp.sum(picked * arc_weight[None, :], axis=1)
    weighted = design[:, :SLAB] * weight[:, None]
    normal_sum = lax.dot_general(weighted, design, (((0,), (0,)), ((), ())),
                                 precision=lax.Precision.HIGHEST, preferred_element_type=jnp.float32)
    rhs_sum = jnp.dot(weight * observed, design, precision=lax.Precision.HIGHEST,
                      preferred_element_type=jnp.float32)
    return normal_sum.reshape(RT, N_ROW * NB, CT, N_COL * NB), rhs_sum.reshape(CT, N_COL, NB)
```

```python
import functools
import jax
import jax.numpy as jnp
from jax import lax
from jax.experimental import pallas as pl
from jax.experimental.pallas import tpu as pltpu
from jax.sharding import PartitionSpec as P

RT = 4
LANES = 128
MESH = pl.DeviceIdType.MESH


def gather_kernel(
    sizes,
    arc_weight, start, cosine, arc_index, observed, gain, damp, orient,
    split_out, lhs_hi, lhs_lo, rhs_out,
    every, split, forcing, f_t, g_t, d_t, q_t, slab, wsend, wblocks, wcol, ocol,
    fsem, osem, rsem, xsem, wrsem, slsem, up_sem, down_sem, y_sem, x_send, w_send, sl_send,
):
    rows, cols, tiles, obs = sizes
    line = rows // 2
    per = LANES // obs
    half = per // 2
    chunks = tiles // per
    r = lax.axis_index("row")
    c = lax.axis_index("col")
    u = r // 2
    v = r % 2
    even = u % 2 == 0
    mate = u + 1 - 2 * (u % 2)
    owner = r % cols
    stride = rows // cols
    slab_chunk = ((RT - 1) * stride + stride - 1) // per

    def row_of(uu, vv):
        return uu * 2 + vv

    barrier = pltpu.get_barrier_semaphore()
    for d in range(1, rows):
        pl.semaphore_signal(barrier, inc=1, device_id=((r + d) % rows, c), device_id_type=MESH)
    for d in range(1, cols):
        pl.semaphore_signal(barrier, inc=1, device_id=(r, (c + d) % cols), device_id_type=MESH)

    def fetch(j):
        return pltpu.make_async_copy(orient.at[:, j, 0, :], forcing.at[j], fsem.at[j])

    @pl.loop(0, tiles)
    def _(j):
        fetch(j).start()

    index = arc_index[...]
    weight = jnp.zeros(index.shape, jnp.float32)
    for k in range(arc_weight.shape[0]):
        weight = weight + jnp.where(index == k, arc_weight[k], 0.0)
    wsend[...] = jnp.zeros_like(wsend)
    wsend[0:1, 0:obs] = weight
    wsend[1:2, 0:obs] = weight * observed[...]
    cos_row = jnp.concatenate([cosine[...]] * per, axis=1)

    def block(t, src, low=0, count=per):
        return every.at[pl.ds(t * per + low, count), pl.ds(pl.multiple_of(src * obs, obs), obs), :]

    def send(t, src, to_row, send_sem, recv_sem, low=0, count=per):
        pltpu.make_async_remote_copy(
            src_ref=block(t, src, low, count),
            dst_ref=block(t, src, low, count),
            send_sem=send_sem,
            recv_sem=recv_sem,
            device_id=(to_row, c),
            device_id_type=MESH,
        ).start()

    def arrived(t, src, sem, low=0, count=per):
        ref = block(t, src, low, count)
        pltpu.make_async_copy(ref, ref, sem).wait()

    def slab_tile(i):
        return i * stride + r // cols

    def relay(t, src):
        @pl.when((t == slab_chunk) & (c == owner))
        def _():
            spot = pl.ds(pl.multiple_of(src * obs, obs), obs)

            @pl.loop(0, RT)
            def _(i):
                for d in range(1, cols):
                    pltpu.make_async_remote_copy(
                        src_ref=every.at[slab_tile(i), spot, :],
                        dst_ref=slab.at[i, spot, :],
                        send_sem=sl_send.at[d],
                        recv_sem=slsem.at[i, src],
                        device_id=(r, (c + d) % cols),
                        device_id_type=MESH,
                    ).start()

    def columns(ref, t):
        parts = [jnp.broadcast_to(ref[t * per + q, pl.ds(c, 1), :], (obs, LANES)) for q in range(per)]
        return jnp.concatenate(parts, axis=0).T

    def recurrence(t):
        for q in range(per):
            fetch(t * per + q).wait()
        f_t[...] = forcing[pl.ds(t * per, per)].reshape(LANES, LANES).T
        g_t[...] = columns(gain, t) * cos_row
        d_t[...] = columns(damp, t)
        first = jnp.concatenate([start[t * per + q, 0, 0:1, :] for q in range(per)], axis=1)
        second = jnp.concatenate([start[t * per + q, 0, 1:2, :] for q in range(per)], axis=1)

        def step(m, state):
            prev_two, prev_one = state
            for k in range(8):
                at = pl.ds(m * 8 + k, 1)
                current = g_t[at, :] * prev_one + (f_t[at, :] - d_t[at, :] * prev_two)
                q_t[at, :] = current
                prev_two, prev_one = prev_one, current
            return prev_two, prev_one

        lax.fori_loop(0, LANES // 8, step, (first, second))
        own = pl.ds(pl.multiple_of(r * obs, obs), obs)
        every[pl.ds(t * per, per), own, :] = q_t[...].T.reshape(per, obs, LANES)

    def own_sends(t):
        @pl.when(u < line - 1)
        def _():
            send(t, r, row_of(u + 1, v), up_sem.at[0], rsem.at[r, t])

        @pl.when(u > 0)
        def _():
            send(t, r, row_of(u - 1, v), down_sem.at[0], rsem.at[r, t])

        send(t, r, row_of(u, 1 - v), y_sem.at[0], rsem.at[r, t])
        relay(t, r)

    recurrence(0)
    pl.semaphore_wait(barrier, rows - 1 + cols - 1)
    for d in range(1, rows):
        pltpu.make_async_remote_copy(
            src_ref=wsend,
            dst_ref=wblocks.at[r],
            send_sem=w_send.at[d],
            recv_sem=wrsem.at[r],
            device_id=((r + d) % rows, c),
            device_id_type=MESH,
        ).start()
    wblocks[r] = wsend[...]
    own_sends(0)

    @pl.loop(1, chunks)
    def _(t):
        recurrence(t)
        own_sends(t)

    for p in range(1, line):
        @pl.loop(0, chunks)
        def _(t, p=p):
            @pl.when(u >= p)
            def _():
                src = row_of(u - p, v)
                arrived(t, src, rsem.at[src, t])

                @pl.when(u < line - 1)
                def _():
                    send(t, src, row_of(u + 1, v), up_sem.at[p], rsem.at[src, t])

                def whole():
                    send(t, src, row_of(u, 1 - v), y_sem.at[p], rsem.at[src, t])

                if p == 1:
                    pl.when(even)(whole)

                    @pl.when(jnp.logical_not(even))
                    def _():
                        send(t, src, row_of(u, 1 - v), y_sem.at[p], rsem.at[src, t], half, per - half)
                else:
                    whole()
                relay(t, src)

            @pl.when(u + p < line)
            def _():
                src = row_of(u + p, v)
                arrived(t, src, rsem.at[src, t])

                @pl.when(u > 0)
                def _():
                    send(t, src, row_of(u - 1, v), down_sem.at[p], rsem.at[src, t])

                def whole():
                    send(t, src, row_of(u, 1 - v), y_sem.at[line + p], rsem.at[src, t])

                if p == 1:
                    pl.when(jnp.logical_not(even))(whole)

                    @pl.when(even)
                    def _():
                        send(t, src, row_of(u, 1 - v), y_sem.at[line + p], rsem.at[src, t], half, per - half)
                else:
                    whole()
                relay(t, src)

    across = row_of(u, 1 - v)

    @pl.loop(0, chunks)
    def _(t):
        arrived(t, across, rsem.at[across, t])
        send(t, across, row_of(mate, v), x_send, xsem.at[t], 0, half)
        relay(t, across)

    for d in range(1, rows):
        src = (r + d) % rows
        pltpu.make_async_copy(wblocks.at[src], wblocks.at[src], wrsem.at[src]).wait()

    @pl.loop(0, rows)
    def _(src):
        turned = wblocks[src].T
        spot = pl.ds(pl.multiple_of(src * obs, obs), obs)
        wcol[spot, :] = jnp.broadcast_to(turned[0:obs, 0:1], (obs, LANES))
        ocol[spot, :] = jnp.broadcast_to(turned[0:obs, 1:2], (obs, LANES))

    total = rows * obs

    def put(t):
        spot = pl.ds(t * per, per)
        return pltpu.make_async_copy(split.at[spot], split_out.at[spot], osem.at[t])

    @pl.loop(0, chunks)
    def _(t):
        for p in range(1, line):
            for sign in (-1, 1):
                far = u + sign * p

                @pl.when((far >= 0) & (far < line))
                def _(p=p, far=far):
                    src = row_of(far, 1 - v)
                    if p == 1:
                        @pl.when(far == mate)
                        def _():
                            arrived(t, src, rsem.at[src, t], half, per - half)
                            arrived(t, src, xsem.at[t], 0, half)

                        @pl.when(far != mate)
                        def _():
                            arrived(t, src, rsem.at[src, t])
                    else:
                        arrived(t, src, rsem.at[src, t])
                    relay(t, src)

        @pl.loop(0, per)
        def _(q):
            j = t * per + q
            values = every[j]
            rhs_out[pl.ds(j, 1), :] = jnp.sum(values * ocol[...], axis=0, keepdims=True)
            high = values.astype(jnp.bfloat16)
            split[j, 0:total, :] = high
            split[j, total:2 * total, :] = (values - high.astype(jnp.float32)).astype(jnp.bfloat16)

        put(t).start()

    @pl.when(c == owner)
    def _():
        @pl.loop(0, RT)
        def _(i):
            slab[i] = every[slab_tile(i)]

    @pl.when(c != owner)
    def _():
        @pl.loop(0, rows)
        def _(src):
            @pl.loop(0, RT)
            def _(i):
                ref = slab.at[i, pl.ds(pl.multiple_of(src * obs, obs), obs), :]
                pltpu.make_async_copy(ref, ref, slsem.at[i, src]).wait()

    for i in range(RT):
        turned = (slab[i] * wcol[...]).T
        high = turned.astype(jnp.bfloat16)
        at = slice(i * LANES, (i + 1) * LANES)
        lhs_hi[at, 0:total] = high
        lhs_hi[at, total:2 * total] = high
        lhs_lo[at, :] = (turned - high.astype(jnp.float32)).astype(jnp.bfloat16)

    def left(sem, low=0, count=tiles):
        ref = every.at[pl.ds(low, count), pl.ds(0, obs), :]
        pltpu.make_async_copy(ref, ref, sem).wait()

    for p in range(line):
        pl.when((u >= p) & (u < line - 1))(functools.partial(left, up_sem.at[p]))
        pl.when((u + p < line) & (u > 0))(functools.partial(left, down_sem.at[p]))
    left(y_sem.at[0])
    part = chunks * (per - half)
    for p in range(1, line):
        if p == 1:
            pl.when((u >= p) & even)(functools.partial(left, y_sem.at[p]))
            pl.when((u >= p) & jnp.logical_not(even))(functools.partial(left, y_sem.at[p], 0, part))
            pl.when((u + p < line) & jnp.logical_not(even))(functools.partial(left, y_sem.at[line + p]))
            pl.when((u + p < line) & even)(functools.partial(left, y_sem.at[line + p], 0, part))
        else:
            pl.when(u >= p)(functools.partial(left, y_sem.at[p]))
            pl.when(u + p < line)(functools.partial(left, y_sem.at[line + p]))
    left(x_send, 0, chunks * half)
    for d in range(1, rows):
        pltpu.make_async_copy(wsend, wsend, w_send.at[d]).wait()

    @pl.when(c == owner)
    def _():
        for d in range(1, cols):
            pltpu.make_async_copy(slab, slab, sl_send.at[d]).wait()

    @pl.loop(0, chunks)
    def _(t):
        put(t).wait()


def gather(sizes, *operands):
    rows, cols, tiles, obs = sizes
    total = rows * obs
    per = LANES // obs
    chunks = tiles // per
    line = rows // 2
    vmem = pl.BlockSpec(memory_space=pltpu.VMEM)
    anywhere = pl.BlockSpec(memory_space=pl.ANY)
    smem = pl.BlockSpec(memory_space=pltpu.SMEM)
    dma = pltpu.SemaphoreType.DMA
    square = pltpu.VMEM((LANES, LANES), jnp.float32)
    return pl.pallas_call(
        functools.partial(gather_kernel, sizes),
        out_shape=(
            jax.ShapeDtypeStruct((tiles, 2 * total, LANES), jnp.bfloat16),
            jax.ShapeDtypeStruct((RT * LANES, 2 * total), jnp.bfloat16),
            jax.ShapeDtypeStruct((RT * LANES, total), jnp.bfloat16),
            jax.ShapeDtypeStruct((tiles, LANES), jnp.float32),
        ),
        in_specs=[smem] + [vmem] * 6 + [anywhere],
        out_specs=(anywhere, vmem, vmem, vmem),
        scratch_shapes=[
            pltpu.VMEM((tiles, total, LANES), jnp.float32),
            pltpu.VMEM((tiles, 2 * total, LANES), jnp.bfloat16),
            pltpu.VMEM((tiles, obs, LANES), jnp.float32),
            square, square, square, square,
            pltpu.VMEM((RT, total, LANES), jnp.float32),
            pltpu.VMEM((8, LANES), jnp.float32),
            pltpu.VMEM((rows, 8, LANES), jnp.float32),
            pltpu.VMEM((total, LANES), jnp.float32),
            pltpu.VMEM((total, LANES), jnp.float32),
            dma((tiles,)), dma((chunks,)), dma((rows, chunks)), dma((chunks,)), dma((rows,)),
            dma((RT, rows)), dma((line,)), dma((line,)), dma((2 * line,)), dma(()), dma((rows,)),
            dma((cols,)),
        ],
        compiler_params=pltpu.CompilerParams(
            collective_id=0, has_side_effects=True, vmem_limit_bytes=56 << 20
        ),
        name="gather_design",
    )(*operands)


def multiply_kernel(total, lhs_hi, lhs_lo, split, out):
    count = split.shape[0]
    for j in range(0, count, 2):
        pair = jnp.concatenate([split[j], split[j + 1]], axis=1)
        product = jnp.dot(lhs_hi[...], pair, preferred_element_type=jnp.float32)
        product += jnp.dot(lhs_lo[...], pair[0:total], preferred_element_type=jnp.float32)
        for k in range(2):
            piece = product[:, k * LANES:(k + 1) * LANES]
            out[:, :, j + k, :] = piece.reshape(RT, LANES, LANES)


def multiply(sizes, lhs_hi, lhs_lo, split):
    rows, cols, tiles, obs = sizes
    total = rows * obs
    group = 8
    return pl.pallas_call(
        functools.partial(multiply_kernel, total),
        grid=(pl.cdiv(tiles, group),),
        out_shape=jax.ShapeDtypeStruct((RT, LANES, tiles, LANES), jnp.float32),
        in_specs=[
            pl.BlockSpec(lhs_hi.shape, lambda g: (0, 0)),
            pl.BlockSpec(lhs_lo.shape, lambda g: (0, 0)),
            pl.BlockSpec((group, 2 * total, LANES), lambda g: (g, 0, 0)),
        ],
        out_specs=pl.BlockSpec((RT, LANES, group, LANES), lambda g: (0, 0, g, 0)),
        compiler_params=pltpu.CompilerParams(vmem_limit_bytes=48 << 20),
        name="slab_product",
    )(lhs_hi, lhs_lo, split)


def body(
    start_values, cosine, arc_index, arc_weight, observed, orientation_term, step_gain, step_damp
):
    sizes = (lax.axis_size("row"), lax.axis_size("col"), start_values.shape[0], cosine.shape[0])
    split, lhs_hi, lhs_lo, rhs = gather(
        sizes,
        arc_weight,
        start_values,
        cosine.reshape(1, -1),
        arc_index.reshape(1, -1),
        observed.reshape(1, -1),
        step_gain,
        step_damp,
        orientation_term,
    )
    return multiply(sizes, lhs_hi, lhs_lo, split), rhs.reshape(sizes[2], 1, LANES)


def solution(mesh):
    in_specs = (
        P(None, "col", None, "row"),
        P("row"),
        P("row"),
        P(),
        P("row"),
        P("row", None, "col", None),
        P(),
        P(),
    )
    out_specs = (P(None, "row", None, "col"), P(None, "col", None))
    return jax.shard_map(body, mesh=mesh, in_specs=in_specs, out_specs=out_specs, check_vma=False)
```

```python
import functools
import jax
import jax.numpy as jnp
from jax import lax
from jax.experimental import pallas as pl
from jax.experimental.pallas import tpu as pltpu
from jax.sharding import PartitionSpec as P

RT = 4
FIRST = (2, 3)
BATCH = 6
LANES = 128
MESH = pl.DeviceIdType.MESH


def gather_kernel(
    sizes,
    arc_weight, start, cosine, arc_index, observed, gain, damp, orient,
    split_out, lhs_hi, lhs_lo, rhs_out,
    every, split, forcing, padded, starts, f_t, g_t, d_t, q_t, slab, wsend, wblocks, wcol, ocol,
    fsem, osem, rsem, xsem, wrsem, slsem, up_sem, down_sem, y_sem, x_send, w_send, sl_send,
):
    rows, cols, tiles, obs = sizes
    line = rows // 2
    per = LANES // obs
    half = per // 2
    chunks = tiles // per
    r = lax.axis_index("row")
    c = lax.axis_index("col")
    u = r // 2
    v = r % 2
    even = u % 2 == 0
    mate = u + 1 - 2 * (u % 2)
    owner = r % cols
    stride = rows // cols
    slab_chunk = ((RT - 1) * stride + stride - 1) // per

    def row_of(uu, vv):
        return uu * 2 + vv

    barrier = pltpu.get_barrier_semaphore()
    for d in range(1, rows):
        pl.semaphore_signal(barrier, inc=1, device_id=((r + d) % rows, c), device_id_type=MESH)
    for d in range(1, cols):
        pl.semaphore_signal(barrier, inc=1, device_id=(r, (c + d) % cols), device_id_type=MESH)

    def fetch(j):
        return pltpu.make_async_copy(orient.at[:, j, 0, :], forcing.at[j], fsem.at[j])

    @pl.loop(0, tiles)
    def _(j):
        fetch(j).start()

    index = arc_index[...]
    weight = jnp.zeros(index.shape, jnp.float32)
    for k in range(arc_weight.shape[0]):
        weight = weight + jnp.where(index == k, arc_weight[k], 0.0)
    wsend[...] = jnp.zeros_like(wsend)
    wsend[0:1, 0:obs] = weight
    wsend[1:2, 0:obs] = weight * observed[...]
    cos_row = jnp.concatenate([cosine[...]] * per, axis=1)

    def block(t, src, low=0, count=per):
        return every.at[pl.ds(t * per + low, count), pl.ds(pl.multiple_of(src * obs, obs), obs), :]

    def send(t, src, to_row, send_sem, recv_sem, low=0, count=per):
        pltpu.make_async_remote_copy(
            src_ref=block(t, src, low, count),
            dst_ref=block(t, src, low, count),
            send_sem=send_sem,
            recv_sem=recv_sem,
            device_id=(to_row, c),
            device_id_type=MESH,
        ).start()

    def arrived(t, src, sem, low=0, count=per):
        ref = block(t, src, low, count)
        pltpu.make_async_copy(ref, ref, sem).wait()

    def slab_tile(i):
        return i * stride + r // cols

    def relay(t, src):
        @pl.when((t == slab_chunk) & (c == owner))
        def _():
            spot = pl.ds(pl.multiple_of(src * obs, obs), obs)

            @pl.loop(0, RT)
            def _(i):
                for d in range(1, cols):
                    pltpu.make_async_remote_copy(
                        src_ref=every.at[slab_tile(i), spot, :],
                        dst_ref=slab.at[i, spot, :],
                        send_sem=sl_send.at[d],
                        recv_sem=slsem.at[i, src],
                        device_id=(r, (c + d) % cols),
                        device_id_type=MESH,
                    ).start()

    def columns(ref, t):
        parts = [jnp.broadcast_to(ref[t * per + q, pl.ds(c, 1), :], (obs, LANES)) for q in range(per)]
        return jnp.concatenate(parts, axis=0).T

    def recurrences(t0, count):
        state = []
        for k in range(count):
            t = t0 + k
            for q in range(per):
                fetch(t * per + q).wait()
            f_t[k] = forcing[pl.ds(t * per, per)].reshape(LANES, LANES).T
            g_t[k] = columns(gain, t) * cos_row
            d_t[k] = columns(damp, t)
            for which in range(2):
                rows_of = [starts[which, pl.ds(t * per + q, 1), :] for q in range(per)]
                state.append(jnp.concatenate(rows_of, axis=1))

        def step(m, state):
            state = list(state)
            for i in range(8):
                at = pl.ds(m * 8 + i, 1)
                for k in range(count):
                    prev_two, prev_one = state[2 * k], state[2 * k + 1]
                    current = g_t[k, at, :] * prev_one + (f_t[k, at, :] - d_t[k, at, :] * prev_two)
                    q_t[k, at, :] = current
                    state[2 * k], state[2 * k + 1] = prev_one, current
            return tuple(state)

        lax.fori_loop(0, LANES // 8, step, tuple(state))
        own = pl.ds(pl.multiple_of(r * obs, obs), obs)
        for k in range(count):
            t = t0 + k
            every[pl.ds(t * per, per), own, :] = q_t[k].T.reshape(per, obs, LANES)

    def own_sends(t):
        @pl.when(u < line - 1)
        def _():
            send(t, r, row_of(u + 1, v), up_sem.at[0], rsem.at[r, t])

        @pl.when(u > 0)
        def _():
            send(t, r, row_of(u - 1, v), down_sem.at[0], rsem.at[r, t])

        send(t, r, row_of(u, 1 - v), y_sem.at[0], rsem.at[r, t])
        relay(t, r)

    for which in range(2):
        padded[...] = jnp.zeros_like(padded)
        padded[:, 0:tiles] = start[0, which]
        starts[which] = padded[...].T

    begun = FIRST[0]
    recurrences(0, begun)
    pl.semaphore_wait(barrier, rows - 1 + cols - 1)
    for d in range(1, rows):
        pltpu.make_async_remote_copy(
            src_ref=wsend,
            dst_ref=wblocks.at[r],
            send_sem=w_send.at[d],
            recv_sem=wrsem.at[r],
            device_id=((r + d) % rows, c),
            device_id_type=MESH,
        ).start()
    wblocks[r] = wsend[...]
    for t in range(begun):
        own_sends(t)
    while begun < chunks:
        count = min(chunks - begun, FIRST[1] if begun == FIRST[0] else BATCH)
        recurrences(begun, count)

        @pl.loop(begun, begun + count)
        def _(t):
            own_sends(t)

        begun += count

    for p in range(1, line):
        @pl.loop(0, chunks)
        def _(t, p=p):
            @pl.when(u >= p)
            def _():
                src = row_of(u - p, v)
                arrived(t, src, rsem.at[src, t])

                @pl.when(u < line - 1)
                def _():
                    send(t, src, row_of(u + 1, v), up_sem.at[p], rsem.at[src, t])

                def whole():
                    send(t, src, row_of(u, 1 - v), y_sem.at[p], rsem.at[src, t])

                if p == 1:
                    pl.when(even)(whole)

                    @pl.when(jnp.logical_not(even))
                    def _():
                        send(t, src, row_of(u, 1 - v), y_sem.at[p], rsem.at[src, t], half, per - half)
                else:
                    whole()
                relay(t, src)

            @pl.when(u + p < line)
            def _():
                src = row_of(u + p, v)
                arrived(t, src, rsem.at[src, t])

                @pl.when(u > 0)
                def _():
                    send(t, src, row_of(u - 1, v), down_sem.at[p], rsem.at[src, t])

                def whole():
                    send(t, src, row_of(u, 1 - v), y_sem.at[line + p], rsem.at[src, t])

                if p == 1:
                    pl.when(jnp.logical_not(even))(whole)

                    @pl.when(even)
                    def _():
                        send(t, src, row_of(u, 1 - v), y_sem.at[line + p], rsem.at[src, t], half, per - half)
                else:
                    whole()
                relay(t, src)

    across = row_of(u, 1 - v)

    @pl.loop(0, chunks)
    def _(t):
        arrived(t, across, rsem.at[across, t])
        send(t, across, row_of(mate, v), x_send, xsem.at[t], 0, half)
        relay(t, across)

    for d in range(1, rows):
        src = (r + d) % rows
        pltpu.make_async_copy(wblocks.at[src], wblocks.at[src], wrsem.at[src]).wait()

    @pl.loop(0, rows)
    def _(src):
        turned = wblocks[src].T
        spot = pl.ds(pl.multiple_of(src * obs, obs), obs)
        wcol[spot, :] = jnp.broadcast_to(turned[0:obs, 0:1], (obs, LANES))
        ocol[spot, :] = jnp.broadcast_to(turned[0:obs, 1:2], (obs, LANES))

    total = rows * obs

    def put(t):
        spot = pl.ds(t * per, per)
        return pltpu.make_async_copy(split.at[spot], split_out.at[spot], osem.at[t])

    @pl.loop(0, chunks)
    def _(t):
        for p in range(1, line):
            for sign in (-1, 1):
                far = u + sign * p

                @pl.when((far >= 0) & (far < line))
                def _(p=p, far=far):
                    src = row_of(far, 1 - v)
                    if p == 1:
                        @pl.when(far == mate)
                        def _():
                            arrived(t, src, rsem.at[src, t], half, per - half)
                            arrived(t, src, xsem.at[t], 0, half)

                        @pl.when(far != mate)
                        def _():
                            arrived(t, src, rsem.at[src, t])
                    else:
                        arrived(t, src, rsem.at[src, t])
                    relay(t, src)

        @pl.loop(0, per)
        def _(q):
            j = t * per + q
            values = every[j]
            rhs_out[j] = jnp.sum(values * ocol[...], axis=0, keepdims=True)
            high = values.astype(jnp.bfloat16)
            split[j, 0:total, :] = high
            split[j, total:2 * total, :] = (values - high.astype(jnp.float32)).astype(jnp.bfloat16)

        put(t).start()

    @pl.when(c == owner)
    def _():
        @pl.loop(0, RT)
        def _(i):
            slab[i] = every[slab_tile(i)]

    @pl.when(c != owner)
    def _():
        @pl.loop(0, rows)
        def _(src):
            @pl.loop(0, RT)
            def _(i):
                ref = slab.at[i, pl.ds(pl.multiple_of(src * obs, obs), obs), :]
                pltpu.make_async_copy(ref, ref, slsem.at[i, src]).wait()

    for i in range(RT):
        turned = (slab[i] * wcol[...]).T
        high = turned.astype(jnp.bfloat16)
        at = slice(i * LANES, (i + 1) * LANES)
        lhs_hi[at, 0:total] = high
        lhs_hi[at, total:2 * total] = high
        lhs_lo[at, :] = (turned - high.astype(jnp.float32)).astype(jnp.bfloat16)

    def left(sem, low=0, count=tiles):
        ref = every.at[pl.ds(low, count), pl.ds(0, obs), :]
        pltpu.make_async_copy(ref, ref, sem).wait()

    for p in range(line):
        pl.when((u >= p) & (u < line - 1))(functools.partial(left, up_sem.at[p]))
        pl.when((u + p < line) & (u > 0))(functools.partial(left, down_sem.at[p]))
    left(y_sem.at[0])
    part = chunks * (per - half)
    for p in range(1, line):
        if p == 1:
            pl.when((u >= p) & even)(functools.partial(left, y_sem.at[p]))
            pl.when((u >= p) & jnp.logical_not(even))(functools.partial(left, y_sem.at[p], 0, part))
            pl.when((u + p < line) & jnp.logical_not(even))(functools.partial(left, y_sem.at[line + p]))
            pl.when((u + p < line) & even)(functools.partial(left, y_sem.at[line + p], 0, part))
        else:
            pl.when(u >= p)(functools.partial(left, y_sem.at[p]))
            pl.when(u + p < line)(functools.partial(left, y_sem.at[line + p]))
    left(x_send, 0, chunks * half)
    for d in range(1, rows):
        pltpu.make_async_copy(wsend, wsend, w_send.at[d]).wait()

    @pl.when(c == owner)
    def _():
        for d in range(1, cols):
            pltpu.make_async_copy(slab, slab, sl_send.at[d]).wait()

    @pl.loop(0, chunks)
    def _(t):
        put(t).wait()


def gather(sizes, *operands):
    rows, cols, tiles, obs = sizes
    total = rows * obs
    per = LANES // obs
    chunks = tiles // per
    line = rows // 2
    vmem = pl.BlockSpec(memory_space=pltpu.VMEM)
    anywhere = pl.BlockSpec(memory_space=pl.ANY)
    smem = pl.BlockSpec(memory_space=pltpu.SMEM)
    dma = pltpu.SemaphoreType.DMA
    squares = pltpu.VMEM((BATCH, LANES, LANES), jnp.float32)
    return pl.pallas_call(
        functools.partial(gather_kernel, sizes),
        out_shape=(
            jax.ShapeDtypeStruct((tiles, 2 * total, LANES), jnp.bfloat16),
            jax.ShapeDtypeStruct((RT * LANES, 2 * total), jnp.bfloat16),
            jax.ShapeDtypeStruct((RT * LANES, total), jnp.bfloat16),
            jax.ShapeDtypeStruct((tiles, 1, LANES), jnp.float32),
        ),
        in_specs=[smem] + [vmem] * 6 + [anywhere],
        out_specs=(anywhere, vmem, vmem, vmem),
        scratch_shapes=[
            pltpu.VMEM((tiles, total, LANES), jnp.float32),
            pltpu.VMEM((tiles, 2 * total, LANES), jnp.bfloat16),
            pltpu.VMEM((tiles, obs, LANES), jnp.float32),
            pltpu.VMEM((obs, LANES), jnp.float32),
            pltpu.VMEM((2, LANES, obs), jnp.float32),
            squares, squares, squares, squares,
            pltpu.VMEM((RT, total, LANES), jnp.float32),
            pltpu.VMEM((8, LANES), jnp.float32),
            pltpu.VMEM((rows, 8, LANES), jnp.float32),
            pltpu.VMEM((total, LANES), jnp.float32),
            pltpu.VMEM((total, LANES), jnp.float32),
            dma((tiles,)), dma((chunks,)), dma((rows, chunks)), dma((chunks,)), dma((rows,)),
            dma((RT, rows)), dma((line,)), dma((line,)), dma((2 * line,)), dma(()), dma((rows,)),
            dma((cols,)),
        ],
        compiler_params=pltpu.CompilerParams(
            collective_id=0, has_side_effects=True, vmem_limit_bytes=56 << 20
        ),
        name="gather_design",
    )(*operands)


def multiply_kernel(total, lhs_hi, lhs_lo, split, rhs, out, rhs_out):
    rhs_out[...] = rhs[...]
    for j in range(0, split.shape[0], 2):
        pair = jnp.concatenate([split[j], split[j + 1]], axis=1)
        product = jnp.dot(lhs_hi[...], pair, preferred_element_type=jnp.float32)
        product += jnp.dot(lhs_lo[...], pair[0:total], preferred_element_type=jnp.float32)
        for k in range(2):
            piece = product[:, k * LANES:(k + 1) * LANES]
            out[:, j + k] = piece.reshape(RT, LANES, LANES)


def multiply(sizes, lhs_hi, lhs_lo, split, rhs):
    rows, cols, tiles, obs = sizes
    total = rows * obs
    group = 4
    return pl.pallas_call(
        functools.partial(multiply_kernel, total),
        grid=(tiles // group,),
        out_shape=(
            jax.ShapeDtypeStruct((RT, tiles, LANES, LANES), jnp.float32),
            jax.ShapeDtypeStruct(rhs.shape, jnp.float32),
        ),
        in_specs=[
            pl.BlockSpec(lhs_hi.shape, lambda g: (0, 0)),
            pl.BlockSpec(lhs_lo.shape, lambda g: (0, 0)),
            pl.BlockSpec((group, 2 * total, LANES), lambda g: (g, 0, 0)),
            pl.BlockSpec((group, 1, LANES), lambda g: (g, 0, 0)),
        ],
        out_specs=(
            pl.BlockSpec((RT, group, LANES, LANES), lambda g: (0, g, 0, 0)),
            pl.BlockSpec((group, 1, LANES), lambda g: (g, 0, 0)),
        ),
        compiler_params=pltpu.CompilerParams(vmem_limit_bytes=60 << 20),
        name="slab_product",
    )(lhs_hi, lhs_lo, split, rhs)


def body(
    start_values, cosine, arc_index, arc_weight, observed, orientation_term, step_gain, step_damp
):
    sizes = (lax.axis_size("row"), lax.axis_size("col"), start_values.shape[0], cosine.shape[0])
    split, lhs_hi, lhs_lo, rhs = gather(
        sizes,
        arc_weight,
        jnp.transpose(start_values, (1, 2, 3, 0)),
        cosine.reshape(1, -1),
        arc_index.reshape(1, -1),
        observed.reshape(1, -1),
        step_gain,
        step_damp,
        orientation_term,
    )
    normal, rhs = multiply(sizes, lhs_hi, lhs_lo, split, rhs)
    return jnp.transpose(normal, (0, 2, 1, 3)), rhs


def solution(mesh):
    in_specs = (
        P(None, "col", None, "row"),
        P("row"),
        P("row"),
        P(),
        P("row"),
        P("row", None, "col", None),
        P(),
        P(),
    )
    out_specs = (P(None, "row", None, "col"), P(None, "col", None))
    return jax.shard_map(body, mesh=mesh, in_specs=in_specs, out_specs=out_specs, check_vma=False)
```

```python
import functools
import jax
import jax.numpy as jnp
from jax import lax
from jax.experimental import pallas as pl
from jax.experimental.pallas import tpu as pltpu
from jax.sharding import PartitionSpec as P

RT = 4
FIRST = (2, 3)
BATCH = 6
LANES = 128
MESH = pl.DeviceIdType.MESH


def gather_kernel(
    sizes,
    arc_weight_in, start_in, cosine_in, arc_index_in, observed_in, gain_in, damp_in, orient,
    split, hi, rhs_out,
    arc_weight, start, cosine, arc_index, observed, gain, damp,
    every, forcing, padded, starts, f_t, g_t, d_t, q_t, slab, wsend, wblocks, wcol, ocol,
    isem, fsem, rsem, xsem, wrsem, slsem, up_sem, down_sem, y_sem, x_send, w_send, sl_send,
):
    rows, cols, tiles, obs = sizes
    line = rows // 2
    per = LANES // obs
    half = per // 2
    chunks = tiles // per
    r = lax.axis_index("row")
    c = lax.axis_index("col")
    u = r // 2
    v = r % 2
    even = u % 2 == 0
    mate = u + 1 - 2 * (u % 2)
    owner = r % cols
    stride = rows // cols
    slab_chunk = ((RT - 1) * stride + stride - 1) // per

    def row_of(uu, vv):
        return uu * 2 + vv

    inputs = (arc_weight_in, start_in, cosine_in, arc_index_in, observed_in, gain_in, damp_in)
    held = (arc_weight, start, cosine, arc_index, observed, gain, damp)
    loads = [pltpu.make_async_copy(a, b, isem.at[k]) for k, (a, b) in enumerate(zip(inputs, held))]
    for copy in loads:
        copy.start()
    barrier = pltpu.get_barrier_semaphore()
    for d in range(1, rows):
        pl.semaphore_signal(barrier, inc=1, device_id=((r + d) % rows, c), device_id_type=MESH)
    for d in range(1, cols):
        pl.semaphore_signal(barrier, inc=1, device_id=(r, (c + d) % cols), device_id_type=MESH)

    def fetch(j):
        return pltpu.make_async_copy(orient.at[:, j, 0, :], forcing.at[j], fsem.at[j])

    @pl.loop(0, tiles)
    def _(j):
        fetch(j).start()

    for copy in loads:
        copy.wait()
    index = arc_index[...]
    weight = jnp.zeros(index.shape, jnp.float32)
    for k in range(arc_weight.shape[1]):
        weight = weight + jnp.where(index == k, arc_weight[:, k:k + 1], 0.0)
    wsend[...] = jnp.zeros_like(wsend)
    wsend[0:1, 0:obs] = weight
    wsend[1:2, 0:obs] = weight * observed[...]
    cos_row = jnp.concatenate([cosine[...]] * per, axis=1)

    def block(t, src, low=0, count=per):
        return every.at[pl.ds(t * per + low, count), pl.ds(pl.multiple_of(src * obs, obs), obs), :]

    def send(t, src, to_row, send_sem, recv_sem, low=0, count=per):
        pltpu.make_async_remote_copy(
            src_ref=block(t, src, low, count),
            dst_ref=block(t, src, low, count),
            send_sem=send_sem,
            recv_sem=recv_sem,
            device_id=(to_row, c),
            device_id_type=MESH,
        ).start()

    def arrived(t, src, sem, low=0, count=per):
        ref = block(t, src, low, count)
        pltpu.make_async_copy(ref, ref, sem).wait()

    def slab_tile(i):
        return i * stride + r // cols

    def relay(t, src):
        @pl.when((t == slab_chunk) & (c == owner))
        def _():
            spot = pl.ds(pl.multiple_of(src * obs, obs), obs)

            @pl.loop(0, RT)
            def _(i):
                for d in range(1, cols):
                    pltpu.make_async_remote_copy(
                        src_ref=every.at[slab_tile(i), spot, :],
                        dst_ref=slab.at[i, spot, :],
                        send_sem=sl_send.at[d],
                        recv_sem=slsem.at[i, src],
                        device_id=(r, (c + d) % cols),
                        device_id_type=MESH,
                    ).start()

    def columns(ref, t):
        parts = [jnp.broadcast_to(ref[t * per + q, pl.ds(c, 1), :], (obs, LANES)) for q in range(per)]
        return jnp.concatenate(parts, axis=0).T

    def recurrences(t0, count):
        state = []
        for k in range(count):
            t = t0 + k
            for q in range(per):
                fetch(t * per + q).wait()
            f_t[k] = forcing[pl.ds(t * per, per)].reshape(LANES, LANES).T
            g_t[k] = columns(gain, t) * cos_row
            d_t[k] = columns(damp, t)
            for which in range(2):
                rows_of = [starts[which, pl.ds(t * per + q, 1), :] for q in range(per)]
                state.append(jnp.concatenate(rows_of, axis=1))

        def step(m, state):
            state = list(state)
            for i in range(8):
                at = pl.ds(m * 8 + i, 1)
                for k in range(count):
                    prev_two, prev_one = state[2 * k], state[2 * k + 1]
                    current = g_t[k, at, :] * prev_one + (f_t[k, at, :] - d_t[k, at, :] * prev_two)
                    q_t[k, at, :] = current
                    state[2 * k], state[2 * k + 1] = prev_one, current
            return tuple(state)

        lax.fori_loop(0, LANES // 8, step, tuple(state))
        own = pl.ds(pl.multiple_of(r * obs, obs), obs)
        for k in range(count):
            t = t0 + k
            every[pl.ds(t * per, per), own, :] = q_t[k].T.reshape(per, obs, LANES)

    def own_sends(t):
        @pl.when(u < line - 1)
        def _():
            send(t, r, row_of(u + 1, v), up_sem.at[0], rsem.at[r, t])

        @pl.when(u > 0)
        def _():
            send(t, r, row_of(u - 1, v), down_sem.at[0], rsem.at[r, t])

        send(t, r, row_of(u, 1 - v), y_sem.at[0], rsem.at[r, t])
        relay(t, r)

    for which in range(2):
        padded[...] = jnp.zeros_like(padded)
        padded[:, 0:tiles] = start[0, which]
        starts[which] = padded[...].T

    begun = FIRST[0]
    recurrences(0, begun)
    pl.semaphore_wait(barrier, rows - 1 + cols - 1)
    for d in range(1, rows):
        pltpu.make_async_remote_copy(
            src_ref=wsend,
            dst_ref=wblocks.at[r],
            send_sem=w_send.at[d],
            recv_sem=wrsem.at[r],
            device_id=((r + d) % rows, c),
            device_id_type=MESH,
        ).start()
    wblocks[r] = wsend[...]
    for t in range(begun):
        own_sends(t)
    while begun < chunks:
        count = min(chunks - begun, FIRST[1] if begun == FIRST[0] else BATCH)
        recurrences(begun, count)

        @pl.loop(begun, begun + count)
        def _(t):
            own_sends(t)

        begun += count

    for p in range(1, line):
        @pl.loop(0, chunks)
        def _(t, p=p):
            @pl.when(u >= p)
            def _():
                src = row_of(u - p, v)
                arrived(t, src, rsem.at[src, t])

                @pl.when(u < line - 1)
                def _():
                    send(t, src, row_of(u + 1, v), up_sem.at[p], rsem.at[src, t])

                def whole():
                    send(t, src, row_of(u, 1 - v), y_sem.at[p], rsem.at[src, t])

                if p == 1:
                    pl.when(even)(whole)

                    @pl.when(jnp.logical_not(even))
                    def _():
                        send(t, src, row_of(u, 1 - v), y_sem.at[p], rsem.at[src, t], half, per - half)
                else:
                    whole()
                relay(t, src)

            @pl.when(u + p < line)
            def _():
                src = row_of(u + p, v)
                arrived(t, src, rsem.at[src, t])

                @pl.when(u > 0)
                def _():
                    send(t, src, row_of(u - 1, v), down_sem.at[p], rsem.at[src, t])

                def whole():
                    send(t, src, row_of(u, 1 - v), y_sem.at[line + p], rsem.at[src, t])

                if p == 1:
                    pl.when(jnp.logical_not(even))(whole)

                    @pl.when(even)
                    def _():
                        send(t, src, row_of(u, 1 - v), y_sem.at[line + p], rsem.at[src, t], half, per - half)
                else:
                    whole()
                relay(t, src)

    across = row_of(u, 1 - v)

    @pl.loop(0, chunks)
    def _(t):
        arrived(t, across, rsem.at[across, t])
        send(t, across, row_of(mate, v), x_send, xsem.at[t], 0, half)
        relay(t, across)

    for d in range(1, rows):
        src = (r + d) % rows
        pltpu.make_async_copy(wblocks.at[src], wblocks.at[src], wrsem.at[src]).wait()

    @pl.loop(0, rows)
    def _(src):
        turned = wblocks[src].T
        spot = pl.ds(pl.multiple_of(src * obs, obs), obs)
        wcol[spot, :] = jnp.broadcast_to(turned[0:obs, 0:1], (obs, LANES))
        ocol[spot, :] = jnp.broadcast_to(turned[0:obs, 1:2], (obs, LANES))

    total = rows * obs

    def left_side():
        @pl.when(c == owner)
        def _():
            @pl.loop(0, RT)
            def _(i):
                slab[i] = every[slab_tile(i)]

        @pl.when(c != owner)
        def _():
            @pl.loop(0, rows)
            def _(src):
                @pl.loop(0, RT)
                def _(i):
                    ref = slab.at[i, pl.ds(pl.multiple_of(src * obs, obs), obs), :]
                    pltpu.make_async_copy(ref, ref, slsem.at[i, src]).wait()

        for i in range(RT):
            turned = (slab[i] * wcol[...]).T
            high = turned.astype(jnp.bfloat16)
            at = slice(i * LANES, (i + 1) * LANES)
            hi[at, 0:total] = high
            hi[at, total:2 * total] = high
            hi[at, 2 * total:3 * total] = (turned - high.astype(jnp.float32)).astype(jnp.bfloat16)

    @pl.loop(0, chunks)
    def _(t):
        for p in range(1, line):
            for sign in (-1, 1):
                far = u + sign * p

                @pl.when((far >= 0) & (far < line))
                def _(p=p, far=far):
                    src = row_of(far, 1 - v)
                    if p == 1:
                        @pl.when(far == mate)
                        def _():
                            arrived(t, src, rsem.at[src, t], half, per - half)
                            arrived(t, src, xsem.at[t], 0, half)

                        @pl.when(far != mate)
                        def _():
                            arrived(t, src, rsem.at[src, t])
                    else:
                        arrived(t, src, rsem.at[src, t])
                    relay(t, src)

        pl.when(t == chunks - 1)(left_side)

        @pl.loop(0, per)
        def _(q):
            j = t * per + q
            values = every[j]
            rhs_out[j] = jnp.sum(values * ocol[...], axis=0, keepdims=True)
            high = values.astype(jnp.bfloat16)
            split[j, 0:total, :] = high
            split[j, total:2 * total, :] = (values - high.astype(jnp.float32)).astype(jnp.bfloat16)

    def left(sem, low=0, count=tiles):
        ref = every.at[pl.ds(low, count), pl.ds(0, obs), :]
        pltpu.make_async_copy(ref, ref, sem).wait()

    for p in range(line):
        pl.when((u >= p) & (u < line - 1))(functools.partial(left, up_sem.at[p]))
        pl.when((u + p < line) & (u > 0))(functools.partial(left, down_sem.at[p]))
    left(y_sem.at[0])
    part = chunks * (per - half)
    for p in range(1, line):
        if p == 1:
            pl.when((u >= p) & even)(functools.partial(left, y_sem.at[p]))
            pl.when((u >= p) & jnp.logical_not(even))(functools.partial(left, y_sem.at[p], 0, part))
            pl.when((u + p < line) & jnp.logical_not(even))(functools.partial(left, y_sem.at[line + p]))
            pl.when((u + p < line) & even)(functools.partial(left, y_sem.at[line + p], 0, part))
        else:
            pl.when(u >= p)(functools.partial(left, y_sem.at[p]))
            pl.when(u + p < line)(functools.partial(left, y_sem.at[line + p]))
    left(x_send, 0, chunks * half)
    for d in range(1, rows):
        pltpu.make_async_copy(wsend, wsend, w_send.at[d]).wait()

    @pl.when(c == owner)
    def _():
        for d in range(1, cols):
            pltpu.make_async_copy(slab, slab, sl_send.at[d]).wait()


def gather(sizes, *operands):
    rows, cols, tiles, obs = sizes
    total = rows * obs
    per = LANES // obs
    chunks = tiles // per
    line = rows // 2
    vmem = pl.BlockSpec(memory_space=pltpu.VMEM)
    held = [pltpu.VMEM(x.shape, x.dtype) for x in operands[:-1]]
    dma = pltpu.SemaphoreType.DMA
    squares = pltpu.VMEM((BATCH, LANES, LANES), jnp.float32)
    return pl.pallas_call(
        functools.partial(gather_kernel, sizes),
        out_shape=(
            pltpu.VMEM((tiles, 2 * total, LANES), jnp.bfloat16),
            pltpu.VMEM((RT * LANES, 3 * total), jnp.bfloat16),
            pltpu.VMEM((tiles, 1, LANES), jnp.float32),
        ),
        in_specs=[pl.BlockSpec(memory_space=pltpu.HBM)] * len(operands),
        out_specs=(vmem, vmem, vmem),
        scratch_shapes=[
            *held,
            pltpu.VMEM((tiles, total, LANES), jnp.float32),
            pltpu.VMEM((tiles, obs, LANES), jnp.float32),
            pltpu.VMEM((obs, LANES), jnp.float32),
            pltpu.VMEM((2, LANES, obs), jnp.float32),
            squares, squares, squares, squares,
            pltpu.VMEM((RT, total, LANES), jnp.float32),
            pltpu.VMEM((8, LANES), jnp.float32),
            pltpu.VMEM((rows, 8, LANES), jnp.float32),
            pltpu.VMEM((total, LANES), jnp.float32),
            pltpu.VMEM((total, LANES), jnp.float32),
            dma((len(held),)), dma((tiles,)), dma((rows, chunks)), dma((chunks,)), dma((rows,)),
            dma((RT, rows)), dma((line,)), dma((line,)), dma((2 * line,)), dma(()), dma((rows,)),
            dma((cols,)),
        ],
        compiler_params=pltpu.CompilerParams(
            collective_id=0, has_side_effects=True, vmem_limit_bytes=32 << 20
        ),
        name="gather_design",
    )(*(pltpu.with_memory_space_constraint(x, pltpu.HBM) for x in operands))


def multiply_kernel(group, lhs, held, rhs, out, rhs_out, result, osem):
    tiles, depth, _ = held.shape
    total = depth // 2
    steps = tiles // group

    def store(t):
        spot = pl.ds(t * group, group)
        return pltpu.make_async_copy(result.at[:, spot], out.at[:, spot], osem.at[t])

    @pl.loop(0, steps)
    def _(t):
        for k in range(0, group, 2):
            j = t * group + k
            pair = jnp.concatenate([held[j], held[j + 1]], axis=1)
            depths = jnp.concatenate([pair, pair[0:total]], axis=0)
            product = jnp.dot(lhs[...], depths, preferred_element_type=jnp.float32)
            for n in range(2):
                piece = product[:, n * LANES:(n + 1) * LANES]
                result[:, j + n] = piece.reshape(RT, LANES, LANES)
        store(t).start()

    rhs_out[...] = rhs[...]

    @pl.loop(0, steps)
    def _(t):
        store(t).wait()


def multiply(sizes, lhs, split, rhs):
    tiles = sizes[2]
    group = 4
    steps = tiles // group
    vmem = pl.BlockSpec(memory_space=pltpu.VMEM)
    anywhere = pl.BlockSpec(memory_space=pl.ANY)
    dma = pltpu.SemaphoreType.DMA
    product_shape = (RT, tiles, LANES, LANES)
    return pl.pallas_call(
        functools.partial(multiply_kernel, group),
        out_shape=(
            jax.ShapeDtypeStruct(product_shape, jnp.float32),
            jax.ShapeDtypeStruct(rhs.shape, jnp.float32),
        ),
        in_specs=[vmem, vmem, vmem],
        out_specs=(anywhere, vmem),
        scratch_shapes=[
            pltpu.VMEM(product_shape, jnp.float32),
            dma((steps,)),
        ],
        compiler_params=pltpu.CompilerParams(vmem_limit_bytes=32 << 20),
        name="slab_product",
    )(*(pltpu.with_memory_space_constraint(x, pltpu.VMEM) for x in (lhs, split, rhs)))


def body(
    start_values, cosine, arc_index, arc_weight, observed, orientation_term, step_gain, step_damp
):
    sizes = (lax.axis_size("row"), lax.axis_size("col"), start_values.shape[0], cosine.shape[0])
    split, lhs, rhs = gather(
        sizes,
        arc_weight.reshape(1, -1),
        jnp.transpose(start_values, (1, 2, 3, 0)),
        cosine.reshape(1, -1),
        arc_index.reshape(1, -1),
        observed.reshape(1, -1),
        step_gain,
        step_damp,
        orientation_term,
    )
    normal, rhs = multiply(sizes, lhs, split, rhs)
    return jnp.transpose(normal, (0, 2, 1, 3)), rhs


def solution(mesh):
    in_specs = (
        P(None, "col", None, "row"),
        P("row"),
        P("row"),
        P(),
        P("row"),
        P("row", None, "col", None),
        P(),
        P(),
    )
    out_specs = (P(None, "row", None, "col"), P(None, "col", None))
    return jax.shard_map(body, mesh=mesh, in_specs=in_specs, out_specs=out_specs, check_vma=False)
```
